256 devices in a mesh: ctx: 8 (over y_lo, x), exp: 32 (over z, y_hi, core).
Axes of the slice: x: 4, y: 4 (y_hi: 2, y_lo: 2; y = y_hi * 2 + y_lo), z: 8, core: 2. Of those that a mesh axis runs over, the one named last changes fastest.
Arguments:
- queries: bfloat16 [32, 1024, 4096], P('exp', 'ctx'), may hold values from -48 to 48
- keys: bfloat16 [32, 1024, 256], P('exp', 'ctx'), may hold values from -4 to 4
- values: bfloat16 [32, 1024, 256], P('exp', 'ctx'), may hold values from -6 to 6
- positions: int32 [32, 1024], P('exp', 'ctx'), may hold values from 0 to 65535, as said below
- residual: bfloat16 [32, 1024, 4096], P('exp', 'ctx'), may hold values from -6 to 6
- norm_gain: float32 [4096], replicated, may hold values from 0.25 to 1.75
- expert_ids: int32 [32, 1024, 8], P('exp', 'ctx'), may hold values from 0 to 127, as said below
- route_weights: float32 [32, 1024, 8], P('exp', 'ctx'), may hold values from 0.3 to 1
- w_gate: bfloat16 [32, 4096, 1536], P('exp', None, 'ctx'), may hold values from -0.09375 to 0.09375
- w_up: bfloat16 [32, 4096, 1536], P('exp', None, 'ctx'), may hold values from -0.09375 to 0.09375
- w_down: bfloat16 [32, 1536, 4096], P('exp', None, 'ctx'), may hold values from -0.15625 to 0.15625
Outputs:
- layer_out: bfloat16 [32, 1024, 4096], P('exp', 'ctx')
The draws below stay inside these ranges and needn't reach their ends.
Inputs may be any that keep to these rules, and one draw needn't show every extreme that they name: `positions`: strictly increasing along each sequence. `expert_ids`: A token's 8 ids differ. In each aligned block of 128 tokens of a sequence no id is named by more than 9 tokens.
All inputs are finite; a program needn't handle non-finite values.
Results may differ from the reference program's by a relative error of at most 0.007.
Values may be sent and summed in bfloat16 or wider, within the bound.
No kernel may reach another device: no remote copies, remote signals or barrier semaphores. Data moves between devices by JAX's collectives and lax.ppermute only.
A program may use at most 128 MiB of HBM per device.

```python
import math
import jax
import jax.numpy as jnp
from jax import lax

D = 4096
HEADS = 32
KV_HEADS = 2
HEAD_DIM = 128
FF = 1536
ROUTED = 128
TOP = 8
TOK_DEV = 128
EXPERTS = 32
LENGTH = 1024
SEQS = 32
CAP = 9
N_CTX = 8


def base_keys(key):
    raw = jax.random.normal(jax.random.fold_in(key, 11), (SEQS, LENGTH, KV_HEADS * HEAD_DIM), jnp.float32)
    return jnp.clip(raw, -4.0, 4.0)


def draw_keys(key, part):
    return base_keys(key).astype(jnp.bfloat16)


def draw_queries(key, part):
    raw = jax.random.normal(jax.random.fold_in(key, 12), (SEQS, LENGTH, HEADS * HEAD_DIM), jnp.float32)
    result = jnp.clip(raw, -5.0, 5.0)
    return result.astype(jnp.bfloat16)


def draw_positions(key, part):
    gaps = jax.random.randint(jax.random.fold_in(key, 21), (SEQS, LENGTH), 1, 3, dtype=jnp.int32)
    ends = jax.random.randint(jax.random.fold_in(key, 22), (SEQS, 1), 2 * LENGTH, 65536, dtype=jnp.int32)
    ends = ends.at[0, 0].set(65535)
    running = jnp.cumsum(gaps, axis=1).astype(jnp.int32)
    return (ends - running[:, -1:] + running).astype(jnp.int32)


def draw_expert_ids(key, part):
    blocks = SEQS * LENGTH // TOK_DEV
    mean_count = TOK_DEV * TOP // ROUTED
    full_expert = jax.random.randint(jax.random.fold_in(key, 31), (), 0, EXPERTS, dtype=jnp.int32)
    block_keys = jax.random.split(jax.random.fold_in(key, 32), blocks)

    def one_block(block_key):
        key_order, key_signs, key_runs, key_tokens = jax.random.split(block_key, 4)
        order = jax.random.permutation(key_order, ROUTED).astype(jnp.int32)
        where_full = jnp.argmax(order == full_expert)
        leading = order[0]
        order = order.at[where_full].set(leading).at[0].set(full_expert)
        signs = jax.random.randint(key_signs, (ROUTED,), 0, 2, dtype=jnp.int32)
        signs = signs.at[0].set(1).at[ROUTED - 1].set(0)
        change = signs - jnp.roll(signs, 1)
        counts = (mean_count + jnp.zeros((ROUTED,), jnp.int32).at[order].set(change)).astype(jnp.int32)
        runs = jax.random.permutation(key_runs, ROUTED).astype(jnp.int32)
        ends = jnp.cumsum(counts[runs]).astype(jnp.int32)
        places = jnp.arange(TOK_DEV * TOP, dtype=jnp.int32)
        which = jnp.sum((places[:, None] >= ends[None, :]).astype(jnp.int32), axis=1)
        expert_at = runs[which]
        table = expert_at.reshape(TOP, TOK_DEV).T
        shuffle = jax.random.permutation(key_tokens, TOK_DEV).astype(jnp.int32)
        return table[shuffle]
    chosen = jax.vmap(one_block)(block_keys)
    return chosen.reshape(SEQS, LENGTH, TOP).astype(jnp.int32)


def levels(rng, dims, cuts, least, high):
    factor_of = 1.0
    for position, parts in cuts:
        steps = jax.random.uniform(jax.random.fold_in(jax.random.fold_in(rng, 6), position), (parts,), jnp.float32, least / len(cuts), high / len(cuts))
        factor_of = factor_of * jnp.repeat(jnp.exp(steps), dims[position] // parts).reshape((-1,) + (1,) * (len(dims) - 1 - position))
    return factor_of


def centred(key, dims, scale, bound, cuts=(), kind=jnp.bfloat16):
    values = scale * jax.random.normal(key, dims, jnp.float32)
    if cuts:
        values = values * levels(key, dims, cuts, -0.22, 0.18)
    return jnp.clip(values, -bound, bound).astype(kind)


def setup_inputs(seed: int = 0) -> dict:
    arg_keys = jax.random.split(jax.random.key(seed), 12)
    return {
        "queries": draw_queries(jax.random.fold_in(arg_keys[11], 71), 0),
        "keys": draw_keys(jax.random.fold_in(arg_keys[11], 71), 0),
        "values": centred(arg_keys[2], (SEQS, LENGTH, KV_HEADS * HEAD_DIM), 1.0, 6.0, ((0, 32), (1, 8))),
        "positions": draw_positions(jax.random.fold_in(arg_keys[11], 71), 0),
        "residual": centred(arg_keys[4], (SEQS, LENGTH, D), 1.0, 6.0, ((0, 32), (1, 8))),
        "norm_gain": jnp.clip(1.0 + 0.15 * jax.random.normal(arg_keys[5], (D,), jnp.float32), 0.25, 1.75),
        "expert_ids": draw_expert_ids(jax.random.fold_in(arg_keys[11], 71), 0),
        "route_weights": jnp.clip(0.3 + 0.7 * jax.random.uniform(arg_keys[7], (SEQS, LENGTH, TOP), jnp.float32) ** levels(arg_keys[7], (SEQS, LENGTH, TOP), ((0, 32), (1, 8)), -0.2, 0.2), 0.3, 1.0),
        "w_gate": centred(arg_keys[8], (EXPERTS, D, FF), D ** -0.5, 0.09375, ((0, 32), (2, 8))),
        "w_up": centred(arg_keys[9], (EXPERTS, D, FF), D ** -0.5, 0.09375, ((0, 32), (2, 8))),
        "w_down": centred(arg_keys[10], (EXPERTS, FF, D), FF ** -0.5, 0.15625, ((0, 32), (2, 8))),
    }


def yarn_tables(position_values):
    half = HEAD_DIM // 2
    theta_base = 1000000.0
    factor = 4.0
    trained_span = 32768.0

    def bound_dim(turns):
        return HEAD_DIM * math.log(trained_span / (turns * 2 * math.pi)) / (2 * math.log(theta_base))
    lower = max(math.floor(bound_dim(32.0)), 0)
    upper = min(math.ceil(bound_dim(1.0)), HEAD_DIM - 1)
    pair_index = jnp.arange(half, dtype=jnp.float32)
    extrapolated = jnp.exp(-(2.0 * pair_index / HEAD_DIM) * math.log(theta_base))
    ramp = jnp.clip((pair_index - lower) / max(upper - lower, 1), 0.0, 1.0)
    inverse = extrapolated / factor * ramp + extrapolated * (1.0 - ramp)
    magnitude = 0.1 * math.log(factor) + 1.0
    angles = position_values.astype(jnp.float32)[..., None] * inverse
    return (jnp.cos(angles) * magnitude, jnp.sin(angles) * magnitude)

def rotate_heads(field, cosine, sine):
    half = HEAD_DIM // 2
    first = field[..., :half]
    second = field[..., half:]
    return jnp.concatenate([first * cosine - second * sine, second * cosine + first * sine], axis=-1)

def attend_sequence(inputs):
    query_rows, key_rows, value_rows, position_row = inputs
    length = query_rows.shape[0]
    group = HEADS // KV_HEADS
    cosine, sine = yarn_tables(position_row)
    cosine = cosine[:, None, :]
    sine = sine[:, None, :]
    q_rot = rotate_heads(query_rows.reshape(length, HEADS, HEAD_DIM).astype(jnp.float32), cosine, sine).astype(jnp.bfloat16)
    k_rot = rotate_heads(key_rows.reshape(length, KV_HEADS, HEAD_DIM).astype(jnp.float32), cosine, sine).astype(jnp.bfloat16)
    grouped = q_rot.reshape(length, KV_HEADS, group, HEAD_DIM).astype(jnp.float32)
    scores = jnp.einsum('tkgd,nkd->kgtn', grouped, k_rot.astype(jnp.float32)) / math.sqrt(HEAD_DIM)
    allowed = position_row[None, :] <= position_row[:, None]
    scores = jnp.where(allowed, scores, jnp.float32(-1e+30))
    largest = lax.optimization_barrier(jnp.max(scores, axis=-1, keepdims=True))
    weight = jnp.where(allowed, jnp.exp(scores - largest), jnp.float32(0.0))
    total = lax.optimization_barrier(jnp.sum(weight, axis=-1))
    weight_b = weight.astype(jnp.bfloat16).astype(jnp.float32)
    value_heads = value_rows.reshape(length, KV_HEADS, HEAD_DIM).astype(jnp.float32)
    mixed = jnp.einsum('kgtn,nkd->kgtd', weight_b, value_heads) / total[..., None]
    return jnp.transpose(mixed, (2, 0, 1, 3)).reshape(length, HEADS * HEAD_DIM)

def reference(queries, keys, values, positions, residual, norm_gain, expert_ids, route_weights, w_gate, w_up, w_down):
    seq_count, length, width = queries.shape
    attn = lax.map(attend_sequence, (queries, keys, values, positions))
    h_state = residual.astype(jnp.float32) + attn
    mean_square = lax.optimization_barrier(jnp.mean(h_state * h_state, axis=-1, keepdims=True))
    normed = (h_state / jnp.sqrt(mean_square + 1e-06) * norm_gain).astype(jnp.bfloat16)
    flat_rows = normed.reshape(seq_count * length, width)
    flat_ids = expert_ids.reshape(-1)
    flat_weights = route_weights.reshape(-1)
    assignments = flat_ids.shape[0]
    most_rows = seq_count * N_CTX * CAP
    choice_index = jnp.arange(assignments, dtype=jnp.int32)

    def add_expert(expert, total):
        chosen = flat_ids == expert
        rank = jnp.cumsum(chosen.astype(jnp.int32)).astype(jnp.int32) - 1
        target = jnp.where(chosen, rank, most_rows).astype(jnp.int32)
        owner = jnp.zeros((most_rows,), jnp.int32).at[target].set(choice_index, mode='drop')
        filled = jnp.zeros((most_rows,), jnp.float32).at[target].set(1.0, mode='drop')
        token_index = (owner // TOP).astype(jnp.int32)
        rows = flat_rows[token_index]
        gate = jnp.dot(rows, w_gate[expert], preferred_element_type=jnp.float32)
        upper = jnp.dot(rows, w_up[expert], preferred_element_type=jnp.float32)
        act = (jax.nn.silu(gate) * upper).astype(jnp.bfloat16)
        out_rows = jnp.dot(act, w_down[expert], preferred_element_type=jnp.float32).astype(jnp.bfloat16)
        scaled = out_rows.astype(jnp.float32) * (flat_weights[owner] * filled)[:, None]
        return total.at[token_index].add(scaled)
    moe_sum = lax.fori_loop(0, EXPERTS, add_expert, jnp.zeros((seq_count * length, width), jnp.float32))
    layer_out = h_state + moe_sum.reshape(seq_count, length, width)
    return layer_out.astype(jnp.bfloat16)
```

```python
import functools
import math

import jax
import jax.numpy as jnp
from jax import lax
from jax.experimental import pallas as pl
from jax.experimental.pallas import tpu as pltpu
from jax.sharding import Mesh
from jax.sharding import PartitionSpec as P

HEADS = 32
KV_HEADS = 2
HEAD_DIM = 128
TOP = 8
HALF = HEAD_DIM // 2
STEP_HEADS = 4
MAIN = 8

F32 = jnp.float32
BF16 = jnp.bfloat16


def yarn_tables(position_values):
    half = HEAD_DIM // 2
    theta_base = 1000000.0
    factor = 4.0
    trained_span = 32768.0

    def bound_dim(turns):
        return (
            HEAD_DIM * math.log(trained_span / (turns * 2 * math.pi)) / (2 * math.log(theta_base))
        )

    lower = max(math.floor(bound_dim(32.0)), 0)
    upper = min(math.ceil(bound_dim(1.0)), HEAD_DIM - 1)
    pair_index = jnp.arange(half, dtype=jnp.float32)
    extrapolated = jnp.exp(-(2.0 * pair_index / HEAD_DIM) * math.log(theta_base))
    ramp = jnp.clip((pair_index - lower) / max(upper - lower, 1), 0.0, 1.0)
    inverse = extrapolated / factor * ramp + extrapolated * (1.0 - ramp)
    magnitude = 0.1 * math.log(factor) + 1.0
    angles = position_values.astype(jnp.float32)[..., None] * inverse
    return (jnp.cos(angles) * magnitude, jnp.sin(angles) * magnitude)


def iota(shape, dim):
    return lax.broadcasted_iota(jnp.int32, shape, dim)


def dot(a, b):
    return jnp.dot(a, b, preferred_element_type=F32)


def rotate(head, cos2, sin2):
    return (head * cos2 + pltpu.roll(head, HALF, 1) * sin2).astype(BF16)


def params(mib):
    return pltpu.CompilerParams(vmem_limit_bytes=mib * 2**20)


def kv_kernel(k_ref, v_ref, cos_ref, sin_ref, kv_ref):
    for head in range(KV_HEADS):
        cols = slice(head * HEAD_DIM, (head + 1) * HEAD_DIM)
        kv_ref[:, cols] = rotate(k_ref[:, cols].astype(F32), cos_ref[...], sin_ref[...])
    kv_ref[:, KV_HEADS * HEAD_DIM :] = v_ref[...]


def pack_kv(keys, values, cos2, sin2):
    tokens, width = keys.shape
    return pl.pallas_call(
        kv_kernel,
        out_shape=jax.ShapeDtypeStruct((tokens, 2 * width), BF16),
        name="pack_kv",
    )(keys, values, cos2, sin2)


def slot_ranks_by_expert(ids_t, experts):
    tokens = ids_t.shape[1]
    expert = iota((experts, tokens), 0)
    named = jnp.zeros((experts, tokens), F32)
    for choice in range(TOP):
        named += (ids_t[choice : choice + 1, :] == expert).astype(F32)
    earlier = (iota((tokens, tokens), 0) < iota((tokens, tokens), 1)).astype(F32)
    rank = dot(named.astype(BF16), earlier.astype(BF16))
    return jnp.where(named > 0.5, rank, 255.0)


def attend_kernel(
    place_ref, q_ref, own_k_ref, own_v_ref, far_k_ref, far_v_ref, cos_ref, sin_ref, residual_ref,
    gain_ref, ids_ref, h_ref, rows_ref,
):
    step = pl.program_id(0)
    tokens = q_ref.shape[0]
    width = h_ref.shape[1]
    cols = STEP_HEADS * HEAD_DIM
    scale = math.log2(math.e) / math.sqrt(HEAD_DIM)
    pieces = []
    for head in range(STEP_HEADS):
        part = q_ref[:, head * HEAD_DIM : (head + 1) * HEAD_DIM].astype(F32)
        pieces.append(rotate(part, cos_ref[...], sin_ref[...]))
    q_rot = jnp.concatenate(pieces, axis=0)
    contract = (((1,), (1,)), ((), ()))
    near = lax.dot_general(q_rot, own_k_ref[...], contract, preferred_element_type=F32)
    far = lax.dot_general(q_rot, far_k_ref[...], contract, preferred_element_type=F32)
    keys = near.shape[1]
    token = iota(near.shape, 0) % tokens
    limit = place_ref[1] * tokens + token
    near = jnp.where(iota(near.shape, 1) <= limit, near, -1e30)
    far = jnp.where(place_ref[0] > 0, far, jnp.full_like(far, -1e30))
    largest = jnp.maximum(
        jnp.max(near, axis=1, keepdims=True), jnp.max(far, axis=1, keepdims=True)
    )
    near = jnp.exp2((near - largest) * scale)
    far = jnp.exp2((far - largest) * scale)
    total = jnp.sum(near, axis=1, keepdims=True) + jnp.sum(far, axis=1, keepdims=True)
    mixed = dot(near.astype(BF16), own_v_ref[...]) + dot(far.astype(BF16), far_v_ref[...])
    attn = mixed / total
    for head in range(STEP_HEADS):
        here = slice(head * HEAD_DIM, (head + 1) * HEAD_DIM)
        start = pl.multiple_of(step * cols + head * HEAD_DIM, HEAD_DIM)
        h_ref[:, pl.ds(start, HEAD_DIM)] = (
            residual_ref[:, here].astype(F32) + attn[head * tokens : (head + 1) * tokens]
        )

    @pl.when(step == pl.num_programs(0) - 1)
    def _():
        experts = rows_ref.shape[0] // MAIN
        slots = rows_ref.shape[0]
        ranks = slot_ranks_by_expert(ids_ref[...], experts)
        spread = (iota((slots, experts), 0) // MAIN == iota((slots, experts), 1)).astype(F32)
        at = dot(spread.astype(BF16), ranks.astype(BF16))
        sub = iota((slots, tokens), 0) % MAIN
        main = (at == sub.astype(F32)).astype(F32).astype(BF16)
        last = at == float(MAIN)
        block = width // MAIN
        square = jnp.zeros((tokens, 1), F32)
        for part in range(MAIN):
            piece = h_ref[:, part * block : (part + 1) * block]
            square += jnp.sum(piece * piece, axis=1, keepdims=True)
        norm = 1.0 / jnp.sqrt(square / width + 1e-06)
        folded = jnp.zeros((slots, block), F32)
        for part in range(MAIN):
            here = slice(part * block, (part + 1) * block)
            normed = (h_ref[:, here] * norm * gain_ref[:, here]).astype(BF16)
            rows_ref[:, here] = dot(main, normed).astype(BF16)
            ninth = (last & (sub == part)).astype(F32).astype(BF16)
            folded += dot(ninth, normed)
        rows_ref[:, width:] = folded.astype(BF16)


def attend(place, queries, own_kv, far_kv, cos2, sin2, residual, gain, ids_t, experts):
    tokens, width = queries.shape
    cols = STEP_HEADS * HEAD_DIM
    steps = width // cols
    per_kv = steps // KV_HEADS
    near = own_kv.shape[0]
    block = width // MAIN
    whole = lambda shape: pl.BlockSpec(shape, lambda i, place: (0,) * len(shape))
    return pl.pallas_call(
        attend_kernel,
        grid_spec=pltpu.PrefetchScalarGridSpec(
            num_scalar_prefetch=1,
            grid=(steps,),
            in_specs=[
                pl.BlockSpec((tokens, cols), lambda i, place: (0, i)),
                pl.BlockSpec((near, HEAD_DIM), lambda i, place: (0, i // per_kv)),
                pl.BlockSpec((near, HEAD_DIM), lambda i, place: (0, KV_HEADS + i // per_kv)),
                pl.BlockSpec((near, HEAD_DIM), lambda i, place: (0, i // per_kv)),
                pl.BlockSpec((near, HEAD_DIM), lambda i, place: (0, KV_HEADS + i // per_kv)),
                whole((tokens, HEAD_DIM)),
                whole((tokens, HEAD_DIM)),
                pl.BlockSpec((tokens, cols), lambda i, place: (0, i)),
                whole((1, width)),
                whole((TOP, tokens)),
            ],
            out_specs=[
                whole((tokens, width)),
                whole((experts * MAIN, width + block)),
            ],
        ),
        out_shape=[
            jax.ShapeDtypeStruct((tokens, width), F32),
            jax.ShapeDtypeStruct((experts * MAIN, width + block), BF16),
        ],
        compiler_params=params(48),
        name="attend",
    )(place, queries, own_kv, own_kv, far_kv, far_kv, cos2, sin2, residual, gain, ids_t)


def gate_up_kernel(rows_ref, weights_ref, act_ref, x_ref):
    slots = rows_ref.shape[0]
    width = x_ref.shape[1]
    experts = slots // MAIN
    block = width // MAIN

    @pl.when(pl.program_id(0) == 0)
    def _():
        x_ref[:slots, :] = rows_ref[:, :width]
        folded = rows_ref[:, width:]
        row, col = iota((experts, slots), 0), iota((experts, slots), 1)
        for part in range(MAIN):
            pick = (col == row * MAIN + part).astype(F32).astype(BF16)
            x_ref[slots:, part * block : (part + 1) * block] = dot(pick, folded).astype(BF16)

    def silu(v):
        return v / (1.0 + jnp.exp(-v))

    tails = []
    for shard in range(2):
        both = dot(x_ref[...], weights_ref[shard])
        gate, upper, tail = both[:, :128], both[:, 128:256], both[:, 256:]
        act_ref[:, shard * 128 : (shard + 1) * 128] = (silu(gate) * upper).astype(BF16)
        tails.append(silu(tail) * pltpu.roll(tail, HALF, 1))
    lane = iota(tails[0].shape, 1)
    act_ref[:, 256:] = jnp.where(lane < HALF, tails[0], pltpu.roll(tails[1], HALF, 1)).astype(BF16)


def gate_up(rows, weights):
    slots, wide = rows.shape
    shards, width, cols = weights.shape
    total = slots + slots // MAIN
    return pl.pallas_call(
        gate_up_kernel,
        grid=(shards // 2,),
        in_specs=[
            pl.BlockSpec((slots, wide), lambda i: (0, 0)),
            pl.BlockSpec((2, width, cols), lambda i: (i, 0, 0)),
        ],
        out_specs=pl.BlockSpec((total, cols), lambda i: (0, i)),
        out_shape=jax.ShapeDtypeStruct((total, cols * shards // 2), BF16),
        scratch_shapes=[pltpu.VMEM((total, width), BF16)],
        compiler_params=params(48),
        cost_estimate=pl.CostEstimate(
            flops=2 * total * width * cols * shards,
            bytes_accessed=2 * weights.size + 4 * rows.size,
            transcendentals=0,
        ),
        name="gate_up",
    )(rows, weights)


def down_kernel(place_ref, own_a, own_b, far_a, far_b, weights_ref, out_ref, fold_ref):
    step = pl.program_id(0)
    slots = out_ref.shape[1]
    experts = slots // MAIN
    cols = weights_ref.shape[3]
    piece = fold_ref.shape[2]
    parts = cols // piece
    mine = place_ref[0]
    first = weights_ref[0, mine]
    second = weights_ref[0, 1 - mine]

    @pl.when(step == 0)
    def _():
        fold_ref[...] = jnp.zeros_like(fold_ref)

    for group, (a, b) in enumerate(((own_a, own_b), (far_a, far_b))):
        to = mine if group == 0 else 1 - mine
        y = (dot(a[...], first) + dot(b[...], second)).astype(BF16)
        start = pl.multiple_of(step * cols, 128)
        out_ref[to, :, pl.ds(start, cols)] = y[:slots]
        row, col = iota((slots, experts), 0), iota((slots, experts), 1)
        for part in range(parts):
            put = (row == col * MAIN + step * parts + part).astype(F32).astype(BF16)
            fold_ref[group] += dot(put, y[slots:, part * piece : (part + 1) * piece])

    @pl.when(step == pl.num_programs(0) - 1)
    def _():
        out_ref[mine, :, out_ref.shape[2] - piece :] = fold_ref[0].astype(BF16)
        out_ref[1 - mine, :, out_ref.shape[2] - piece :] = fold_ref[1].astype(BF16)


def down(place, own_a, own_b, far_a, far_b, weights):
    total, half = own_a.shape
    shards, _, _, cols = weights.shape
    slots = total * MAIN // (MAIN + 1)
    piece = shards * cols // MAIN
    acts = pl.BlockSpec((total, half), lambda i, place: (0, 0))
    return pl.pallas_call(
        down_kernel,
        grid_spec=pltpu.PrefetchScalarGridSpec(
            num_scalar_prefetch=1,
            grid=(shards,),
            in_specs=[acts] * 4
            + [pl.BlockSpec((1, 2, half, cols), lambda i, place: (i, 0, 0, 0))],
            out_specs=pl.BlockSpec((2, slots, shards * cols + piece), lambda i, place: (0, 0, 0)),
            scratch_shapes=[pltpu.VMEM((2, slots, piece), F32)],
        ),
        out_shape=jax.ShapeDtypeStruct((2, slots, shards * cols + piece), BF16),
        compiler_params=params(48),
        name="down",
    )(place, own_a, own_b, far_a, far_b, weights)


def combine_kernel(ids_ref, weights_ref, h_ref, back_ref, out_ref):
    tokens = h_ref.shape[0]
    slots = back_ref.shape[1]
    experts = slots // MAIN
    width = h_ref.shape[1]
    piece = width // MAIN
    expert = iota((tokens, experts), 1)
    named = jnp.zeros((tokens, experts), F32)
    weight = jnp.zeros((tokens, experts), F32)
    for choice in range(TOP):
        match = ids_ref[:, choice : choice + 1] == expert
        named += match.astype(F32)
        weight += jnp.where(match, weights_ref[:, choice : choice + 1], 0.0)
    earlier = (iota((tokens, tokens), 1) < iota((tokens, tokens), 0)).astype(F32)
    rank = jnp.where(named > 0.5, dot(earlier.astype(BF16), named.astype(BF16)), 255.0)
    spread = (iota((experts, slots), 1) // MAIN == iota((experts, slots), 0)).astype(F32)
    spread = spread.astype(BF16)
    at = dot(rank.astype(BF16), spread)
    sub = iota((tokens, slots), 1) % MAIN
    levels = []
    rest = weight
    for _ in range(3):
        level = rest.astype(BF16)
        rest = rest - level.astype(F32)
        levels.append(dot(level, spread))
    main = [jnp.where(at == sub.astype(F32), level, 0.0).astype(BF16) for level in levels]
    last = [jnp.where(at == float(MAIN), level, 0.0) for level in levels]
    main = jnp.concatenate(main, axis=0)

    def add_up(stacked):
        return stacked[:tokens] + (stacked[tokens : 2 * tokens] + stacked[2 * tokens :])

    for part in range(MAIN):
        here = slice(part * piece, (part + 1) * piece)
        ninth = jnp.concatenate(
            [jnp.where(sub == part, level, 0.0).astype(BF16) for level in last], axis=0
        )
        summed = dot(main, back_ref[0, :, here]) + dot(ninth, back_ref[0, :, width:])
        out_ref[:, here] = (h_ref[:, here] + add_up(summed)).astype(BF16)


def combine(ids, weights, h_state, back):
    tokens, width = h_state.shape
    halves, slots, wide = back.shape
    part = width // halves
    return pl.pallas_call(
        combine_kernel,
        grid=(halves,),
        in_specs=[
            pl.BlockSpec((tokens, TOP), lambda i: (0, 0)),
            pl.BlockSpec((tokens, TOP), lambda i: (0, 0)),
            pl.BlockSpec((tokens, part), lambda i: (0, i)),
            pl.BlockSpec((1, slots, wide), lambda i: (i, 0, 0)),
        ],
        out_specs=pl.BlockSpec((tokens, part), lambda i: (0, i)),
        out_shape=jax.ShapeDtypeStruct((tokens, width), BF16),
        compiler_params=params(48),
        name="combine",
    )(ids, weights, h_state, back)


def swap(x):
    return lax.ppermute(x, "y", [(0, 1), (1, 0)])


def per_device(
    queries,
    keys,
    values,
    positions,
    residual,
    norm_gain,
    expert_ids,
    route_weights,
    w_gate,
    w_up,
    w_down,
):
    width = queries.shape[2]
    owners = lax.axis_size("exp")
    place = jnp.stack([lax.axis_index("y"), lax.axis_index("x")]).astype(jnp.int32)

    cosine, sine = yarn_tables(positions[0])
    cos2 = jnp.concatenate([cosine, cosine], axis=1)
    sin2 = jnp.concatenate([-sine, sine], axis=1)
    kv = pack_kv(keys[0], values[0], cos2, sin2)
    own_kv = lax.all_gather(kv, "x", axis=0, tiled=True)
    far_kv = lax.ppermute(own_kv, "y", [(0, 1)])

    gate, upper = w_gate[0], w_up[0]
    both = jnp.concatenate(
        [gate[:, :128], upper[:, :128], gate[:, 128:], upper[:, 128:]], axis=1
    )
    both = lax.all_gather(both, "x", axis=0)
    hidden, cols = w_down.shape[1:]
    lower = w_down[0].reshape(4, 2, hidden // 8, cols)
    lower = jnp.concatenate(
        [lower[:, :, :128].reshape(4, 256, cols), lower[:, :, 128:].reshape(4, 128, cols)], axis=1
    )
    lower = lax.all_gather(lower.reshape(hidden, cols), "x", axis=0)
    lower = lower.reshape(lower.shape[0], 2, hidden // 2, cols)

    h_state, rows = attend(
        place, queries[0], own_kv, far_kv, cos2, sin2, residual[0], norm_gain[None],
        expert_ids[0].T, owners,
    )
    slots = owners * MAIN
    wide = rows.shape[1]
    arrived = lax.all_to_all(
        rows.reshape(owners, MAIN, wide), "exp", split_axis=0, concat_axis=0, tiled=True
    ).reshape(slots, wide)
    passed = swap(arrived)
    own_a = gate_up(arrived, both)
    far_b = swap(own_a)
    far_a = gate_up(passed, both)
    own_b = swap(far_a)
    out = down(place, own_a, own_b, far_a, far_b, lower)
    back = lax.all_to_all(
        out.reshape(2 * owners, MAIN, out.shape[2]),
        ("y", "exp"),
        split_axis=0,
        concat_axis=0,
        tiled=True,
    ).reshape(out.shape)
    return combine(expert_ids[0], route_weights[0], h_state, back)[None]


def solution(mesh):
    inner = Mesh(mesh.devices.reshape(2, 4, mesh.shape["exp"]), ("y", "x", "exp"))
    ctx = ("y", "x")
    return jax.shard_map(
        per_device,
        mesh=inner,
        in_specs=(
            P("exp", ctx, None),
            P("exp", ctx, None),
            P("exp", ctx, None),
            P("exp", ctx),
            P("exp", ctx, None),
            P(),
            P("exp", ctx, None),
            P("exp", ctx, None),
            P("exp", None, ctx),
            P("exp", None, ctx),
            P("exp", None, ctx),
        ),
        out_specs=P("exp", ctx, None),
        check_vma=False,
    )
```

```python
import functools
import math

import jax
import jax.numpy as jnp
from jax import lax
from jax.experimental import pallas as pl
from jax.experimental.pallas import tpu as pltpu
from jax.sharding import Mesh
from jax.sharding import PartitionSpec as P

HEADS = 32
KV_HEADS = 2
HEAD_DIM = 128
TOP = 8
HALF = HEAD_DIM // 2
STEP_HEADS = 4
FIRST = 5
MAIN = 8

F32 = jnp.float32
BF16 = jnp.bfloat16


def yarn_tables(position_values):
    half = HEAD_DIM // 2
    theta_base = 1000000.0
    factor = 4.0
    trained_span = 32768.0

    def bound_dim(turns):
        return (
            HEAD_DIM * math.log(trained_span / (turns * 2 * math.pi)) / (2 * math.log(theta_base))
        )

    lower = max(math.floor(bound_dim(32.0)), 0)
    upper = min(math.ceil(bound_dim(1.0)), HEAD_DIM - 1)
    pair_index = jnp.arange(half, dtype=jnp.float32)
    extrapolated = jnp.exp(-(2.0 * pair_index / HEAD_DIM) * math.log(theta_base))
    ramp = jnp.clip((pair_index - lower) / max(upper - lower, 1), 0.0, 1.0)
    inverse = extrapolated / factor * ramp + extrapolated * (1.0 - ramp)
    magnitude = 0.1 * math.log(factor) + 1.0
    angles = position_values.astype(jnp.float32)[..., None] * inverse
    return (jnp.cos(angles) * magnitude, jnp.sin(angles) * magnitude)


def iota(shape, dim):
    return lax.broadcasted_iota(jnp.int32, shape, dim)


def dot(a, b):
    return jnp.dot(a, b, preferred_element_type=F32)


def rotate(head, cos2, sin2):
    return (head * cos2 + pltpu.roll(head, HALF, 1) * sin2).astype(BF16)


def params(mib):
    return pltpu.CompilerParams(vmem_limit_bytes=mib * 2**20)


def kv_kernel(k_ref, v_ref, cos_ref, sin_ref, kv_ref):
    for head in range(KV_HEADS):
        cols = slice(head * HEAD_DIM, (head + 1) * HEAD_DIM)
        kv_ref[:, cols] = rotate(k_ref[:, cols].astype(F32), cos_ref[...], sin_ref[...])
    kv_ref[:, KV_HEADS * HEAD_DIM :] = v_ref[...]


def pack_kv(keys, values, cos2, sin2):
    tokens, width = keys.shape
    return pl.pallas_call(
        kv_kernel,
        out_shape=jax.ShapeDtypeStruct((tokens, 2 * width), BF16),
        name="pack_kv",
    )(keys, values, cos2, sin2)


def pack_weights_kernel(gate_ref, upper_ref, out_ref):
    both = jnp.concatenate(
        [gate_ref[:128], upper_ref[:128], gate_ref[128:], upper_ref[128:]], axis=0
    )
    out_ref[...] = both.T


def pack_weights(gate, upper):
    units, width = gate.shape
    block = width // 4
    return pl.pallas_call(
        pack_weights_kernel,
        grid=(width // block,),
        in_specs=[pl.BlockSpec((units, block), lambda i: (0, i))] * 2,
        out_specs=pl.BlockSpec((block, 2 * units), lambda i: (i, 0)),
        out_shape=jax.ShapeDtypeStruct((width, 2 * units), BF16),
        name="pack_weights",
    )(gate, upper)


def slot_ranks_by_expert(ids_t, experts):
    tokens = ids_t.shape[1]
    expert = iota((experts, tokens), 0)
    named = jnp.zeros((experts, tokens), F32)
    for choice in range(TOP):
        named += (ids_t[choice : choice + 1, :] == expert).astype(F32)
    earlier = (iota((tokens, tokens), 0) < iota((tokens, tokens), 1)).astype(F32)
    rank = dot(named.astype(BF16), earlier.astype(BF16))
    return jnp.where(named > 0.5, rank, 255.0)


def attend_kernel(
    place_ref, q_ref, own_k_ref, own_v_ref, far_k_ref, far_v_ref, cos_ref, sin_ref, residual_ref,
    gain_ref, ids_ref, h_ref, one_ref, two_ref,
):
    step = pl.program_id(0)
    tokens = q_ref.shape[0]
    width = h_ref.shape[1]
    cols = STEP_HEADS * HEAD_DIM
    scale = math.log2(math.e) / math.sqrt(HEAD_DIM)
    pieces = []
    for head in range(STEP_HEADS):
        part = q_ref[:, head * HEAD_DIM : (head + 1) * HEAD_DIM].astype(F32)
        pieces.append(rotate(part, cos_ref[...], sin_ref[...]))
    q_rot = jnp.concatenate(pieces, axis=0)
    contract = (((1,), (1,)), ((), ()))
    near = lax.dot_general(q_rot, own_k_ref[...], contract, preferred_element_type=F32)
    far = lax.dot_general(q_rot, far_k_ref[...], contract, preferred_element_type=F32)
    keys = near.shape[1]
    token = iota(near.shape, 0) % tokens
    limit = place_ref[1] * tokens + token
    near = jnp.where(iota(near.shape, 1) <= limit, near, -1e30)
    far = jnp.where(place_ref[0] > 0, far, jnp.full_like(far, -1e30))
    largest = jnp.maximum(
        jnp.max(near, axis=1, keepdims=True), jnp.max(far, axis=1, keepdims=True)
    )
    near = jnp.exp2((near - largest) * scale)
    far = jnp.exp2((far - largest) * scale)
    total = jnp.sum(near, axis=1, keepdims=True) + jnp.sum(far, axis=1, keepdims=True)
    mixed = dot(near.astype(BF16), own_v_ref[...]) + dot(far.astype(BF16), far_v_ref[...])
    attn = mixed / total
    for head in range(STEP_HEADS):
        here = slice(head * HEAD_DIM, (head + 1) * HEAD_DIM)
        start = pl.multiple_of(step * cols + head * HEAD_DIM, HEAD_DIM)
        h_ref[:, pl.ds(start, HEAD_DIM)] = (
            residual_ref[:, here].astype(F32) + attn[head * tokens : (head + 1) * tokens]
        )

    @pl.when(step == pl.num_programs(0) - 1)
    def _():
        slots, first = one_ref.shape
        experts = slots // MAIN
        ranks = slot_ranks_by_expert(ids_ref[...], experts)
        spread = (iota((slots, experts), 0) // MAIN == iota((slots, experts), 1)).astype(F32)
        at = dot(spread.astype(BF16), ranks.astype(BF16))
        sub = iota((slots, tokens), 0) % MAIN
        main = (at == sub.astype(F32)).astype(F32).astype(BF16)
        last = at == float(MAIN)
        block = width // MAIN
        square = jnp.zeros((tokens, 1), F32)
        for part in range(MAIN):
            piece = h_ref[:, part * block : (part + 1) * block]
            square += jnp.sum(piece * piece, axis=1, keepdims=True)
        norm = 1.0 / jnp.sqrt(square / width + 1e-06)
        folded = jnp.zeros((slots, block), F32)
        for part in range(MAIN):
            here = slice(part * block, (part + 1) * block)
            normed = (h_ref[:, here] * norm * gain_ref[:, here]).astype(BF16)
            sent = dot(main, normed).astype(BF16)
            if (part + 1) * block <= first:
                one_ref[:, here] = sent
            else:
                two_ref[:, part * block - first : (part + 1) * block - first] = sent
            ninth = (last & (sub == part)).astype(F32).astype(BF16)
            folded += dot(ninth, normed)
        two_ref[:, width - first :] = folded.astype(BF16)


def attend(place, queries, own_kv, far_kv, cos2, sin2, residual, gain, ids_t, experts):
    tokens, width = queries.shape
    cols = STEP_HEADS * HEAD_DIM
    steps = width // cols
    per_kv = steps // KV_HEADS
    near = own_kv.shape[0]
    block = width // MAIN
    first = FIRST * block
    whole = lambda shape: pl.BlockSpec(shape, lambda i, place: (0,) * len(shape))
    return pl.pallas_call(
        attend_kernel,
        grid_spec=pltpu.PrefetchScalarGridSpec(
            num_scalar_prefetch=1,
            grid=(steps,),
            in_specs=[
                pl.BlockSpec((tokens, cols), lambda i, place: (0, i)),
                pl.BlockSpec((near, HEAD_DIM), lambda i, place: (0, i // per_kv)),
                pl.BlockSpec((near, HEAD_DIM), lambda i, place: (0, KV_HEADS + i // per_kv)),
                pl.BlockSpec((near, HEAD_DIM), lambda i, place: (0, i // per_kv)),
                pl.BlockSpec((near, HEAD_DIM), lambda i, place: (0, KV_HEADS + i // per_kv)),
                whole((tokens, HEAD_DIM)),
                whole((tokens, HEAD_DIM)),
                pl.BlockSpec((tokens, cols), lambda i, place: (0, i)),
                whole((1, width)),
                whole((TOP, tokens)),
            ],
            out_specs=[
                whole((tokens, width)),
                whole((experts * MAIN, first)),
                whole((experts * MAIN, width + block - first)),
            ],
        ),
        out_shape=[
            jax.ShapeDtypeStruct((tokens, width), F32),
            jax.ShapeDtypeStruct((experts * MAIN, first), BF16),
            jax.ShapeDtypeStruct((experts * MAIN, width + block - first), BF16),
        ],
        compiler_params=params(48),
        name="attend",
    )(place, queries, own_kv, own_kv, far_kv, far_kv, cos2, sin2, residual, gain, ids_t)


def gate_up_kernel(one_ref, two_ref, weights_ref, act_ref, x_ref, tail_ref):
    slots, first = one_ref.shape
    width = x_ref.shape[1]
    experts = slots // MAIN
    block = width // MAIN
    step = pl.program_id(0)

    @pl.when(step == 0)
    def _():
        x_ref[:slots, :first] = one_ref[...]
        x_ref[:slots, first:] = two_ref[:, : width - first]
        folded = two_ref[:, width - first :]
        row, col = iota((experts, slots), 0), iota((experts, slots), 1)
        for part in range(MAIN):
            pick = (col == row * MAIN + part).astype(F32).astype(BF16)
            x_ref[slots:, part * block : (part + 1) * block] = dot(pick, folded).astype(BF16)

    both = dot(x_ref[...], weights_ref[0])
    gated = (silu(both[:, :128]) * both[:, 128:256]).astype(BF16)
    tail = silu(both[:, 256:]) * pltpu.roll(both[:, 256:], HALF, 1)

    @pl.when(step % 2 == 0)
    def _():
        act_ref[:, :128] = gated
        tail_ref[...] = tail

    @pl.when(step % 2 == 1)
    def _():
        act_ref[:, 128:256] = gated
        lane = iota(tail.shape, 1)
        act_ref[:, 256:] = jnp.where(lane < HALF, tail_ref[...], pltpu.roll(tail, HALF, 1)).astype(
            BF16
        )


def silu(v):
    return v / (1.0 + jnp.exp(-v))


def gate_up(one, two, weights):
    slots = one.shape[0]
    shards, width, cols = weights.shape
    total = slots + slots // MAIN
    return pl.pallas_call(
        gate_up_kernel,
        grid=(shards,),
        in_specs=[
            pl.BlockSpec(one.shape, lambda i: (0, 0)),
            pl.BlockSpec(two.shape, lambda i: (0, 0)),
            pl.BlockSpec((1, width, cols), lambda i: (i, 0, 0)),
        ],
        out_specs=pl.BlockSpec((total, cols), lambda i: (0, i // 2)),
        out_shape=jax.ShapeDtypeStruct((total, cols * shards // 2), BF16),
        scratch_shapes=[pltpu.VMEM((total, width), BF16), pltpu.VMEM((total, 128), F32)],
        compiler_params=params(32),
        cost_estimate=pl.CostEstimate(
            flops=2 * total * width * cols * shards,
            bytes_accessed=2 * weights.size + 2 * (one.size + two.size),
            transcendentals=0,
        ),
        name="gate_up",
    )(one, two, weights)


def down_kernel(
    place_ref, own_a, own_b, far_a, far_b, *refs,
):
    weights, (out_ref, act_ref, fold_ref) = refs[:-3], refs[-3:]
    step = pl.program_id(0)
    slots = out_ref.shape[1]
    experts = slots // MAIN
    total = slots + experts
    cols = weights[0].shape[1]
    piece = fold_ref.shape[2]
    shards = (out_ref.shape[2] - piece) // cols

    @pl.when(step == 0)
    def _():
        row = iota((total, 1), 0)
        block = jnp.where(row < slots, row // MAIN, row - slots)
        mine = (block // 2) % 2 == place_ref[2]
        for half, own, far in ((place_ref[0], own_a, far_a), (1 - place_ref[0], own_b, far_b)):
            near, away = own[...].astype(F32), far[...].astype(F32)
            act_ref[half, :total] = jnp.where(mine, near, away).astype(BF16)
            act_ref[half, total:] = jnp.where(mine, away, near).astype(BF16)
        fold_ref[...] = jnp.zeros_like(fold_ref)

    def in_order(weights):
        rows = []
        for base in range(0, weights.shape[0], 384):
            for start, size in ((0, 128), (192, 128), (128, 64), (320, 64)):
                rows.append(weights[base + start : base + start + size])
        return jnp.concatenate(rows, axis=0)

    def multiply(top, bottom, shard):
        y = dot(act_ref[0], in_order(top)) + dot(act_ref[1], in_order(bottom))
        y = y.astype(BF16)
        start = pl.multiple_of(shard * cols, 128)
        row, col = iota((slots, experts), 0), iota((slots, experts), 1)
        for to in range(2):
            out_ref[to, :, pl.ds(start, cols)] = y[to * total : to * total + slots]
            ninth = y[to * total + slots : (to + 1) * total]
            for part in range(cols // piece):
                at = shard * (cols // piece) + part
                put = (row == col * MAIN + at).astype(F32).astype(BF16)
                fold_ref[to] += dot(put, ninth[:, part * piece : (part + 1) * piece])

    for number, ahead in enumerate((0, shards - 1, 1, 2)):

        @pl.when(step == number)
        def _(number=number, ahead=ahead):
            top, bottom = weights[2 * number : 2 * number + 2]
            multiply(top[...], bottom[...], (place_ref[1] + ahead) % shards)

    @pl.when(step == shards - 1)
    def _():
        for to in range(2):
            out_ref[to, :, out_ref.shape[2] - piece :] = fold_ref[to].astype(BF16)


def down(place, acts, weights):
    total, half = acts[0].shape
    cols = weights[0].shape[1]
    shards = len(weights) // 2
    slots = total * MAIN // (MAIN + 1)
    piece = shards * cols // MAIN
    whole = lambda shape: pl.BlockSpec(shape, lambda i, place: (0,) * len(shape))
    return pl.pallas_call(
        down_kernel,
        grid_spec=pltpu.PrefetchScalarGridSpec(
            num_scalar_prefetch=1,
            grid=(shards,),
            in_specs=[whole(a.shape) for a in (*acts, *weights)],
            out_specs=whole((2, slots, shards * cols + piece)),
            scratch_shapes=[
                pltpu.VMEM((2, 2 * total, half), BF16),
                pltpu.VMEM((2, slots, piece), F32),
            ],
        ),
        out_shape=jax.ShapeDtypeStruct((2, slots, shards * cols + piece), BF16),
        compiler_params=params(36),
        name="down",
    )(place, *acts, *weights)


def combine_kernel(ids_ref, weights_ref, h_ref, back_ref, out_ref):
    tokens = h_ref.shape[0]
    slots = back_ref.shape[1]
    experts = slots // MAIN
    width = h_ref.shape[1]
    piece = width // MAIN
    expert = iota((tokens, experts), 1)
    named = jnp.zeros((tokens, experts), F32)
    weight = jnp.zeros((tokens, experts), F32)
    for choice in range(TOP):
        match = ids_ref[:, choice : choice + 1] == expert
        named += match.astype(F32)
        weight += jnp.where(match, weights_ref[:, choice : choice + 1], 0.0)
    earlier = (iota((tokens, tokens), 1) < iota((tokens, tokens), 0)).astype(F32)
    rank = jnp.where(named > 0.5, dot(earlier.astype(BF16), named.astype(BF16)), 255.0)
    spread = (iota((experts, slots), 1) // MAIN == iota((experts, slots), 0)).astype(F32)
    spread = spread.astype(BF16)
    at = dot(rank.astype(BF16), spread)
    sub = iota((tokens, slots), 1) % MAIN
    levels = []
    rest = weight
    for _ in range(3):
        level = rest.astype(BF16)
        rest = rest - level.astype(F32)
        levels.append(dot(level, spread))
    main = [jnp.where(at == sub.astype(F32), level, 0.0).astype(BF16) for level in levels]
    last = [jnp.where(at == float(MAIN), level, 0.0) for level in levels]
    main = jnp.concatenate(main, axis=0)

    def add_up(stacked):
        return stacked[:tokens] + (stacked[tokens : 2 * tokens] + stacked[2 * tokens :])

    for part in range(MAIN):
        here = slice(part * piece, (part + 1) * piece)
        ninth = jnp.concatenate(
            [jnp.where(sub == part, level, 0.0).astype(BF16) for level in last], axis=0
        )
        summed = dot(main, back_ref[0, :, here]) + dot(ninth, back_ref[0, :, width:])
        out_ref[:, here] = (h_ref[:, here] + add_up(summed)).astype(BF16)


def combine(ids, weights, h_state, back):
    tokens, width = h_state.shape
    halves, slots, wide = back.shape
    part = width // halves
    return pl.pallas_call(
        combine_kernel,
        grid=(halves,),
        in_specs=[
            pl.BlockSpec((tokens, TOP), lambda i: (0, 0)),
            pl.BlockSpec((tokens, TOP), lambda i: (0, 0)),
            pl.BlockSpec((tokens, part), lambda i: (0, i)),
            pl.BlockSpec((1, slots, wide), lambda i: (i, 0, 0)),
        ],
        out_specs=pl.BlockSpec((tokens, part), lambda i: (0, i)),
        out_shape=jax.ShapeDtypeStruct((tokens, width), BF16),
        compiler_params=params(48),
        name="combine",
    )(ids, weights, h_state, back)


def swap(x):
    return lax.ppermute(x, "y", [(0, 1), (1, 0)])


def ring(x, ahead):
    return lax.ppermute(x, "x", [(i, (i + ahead) % 4) for i in range(4)])


def per_device(
    queries,
    keys,
    values,
    positions,
    residual,
    norm_gain,
    expert_ids,
    route_weights,
    w_gate,
    w_up,
    w_down,
):
    width = queries.shape[2]
    owners = lax.axis_size("exp")
    y_high = (lax.axis_index("exp") >> 1) & 1
    place = jnp.stack([lax.axis_index("y"), lax.axis_index("x"), lax.axis_index("y") ^ y_high])
    place = place.astype(jnp.int32)

    cosine, sine = yarn_tables(positions[0])
    cos2 = jnp.concatenate([cosine, cosine], axis=1)
    sin2 = jnp.concatenate([-sine, sine], axis=1)
    kv = pack_kv(keys[0], values[0], cos2, sin2)
    own_kv = lax.all_gather(kv, "x", axis=0, tiled=True)
    far_kv = lax.ppermute(own_kv, "y", [(0, 1)])

    both = pack_weights(w_gate[0].T, w_up[0].T)
    both = lax.all_gather(both, "x", axis=0, tiled=True).reshape(4, width, both.shape[1])
    hidden, cols = w_down.shape[1:]
    here = (w_down[0, : hidden // 2], w_down[0, hidden // 2 :])
    left_top, right_bottom = ring(here[0], 1), ring(here[1], -1)
    left_bottom, right_top = ring(here[1], 1), ring(here[0], -1)

    h_state, one, two = attend(
        place, queries[0], own_kv, far_kv, cos2, sin2, residual[0], norm_gain[None],
        expert_ids[0].T, owners,
    )

    groups = [
        [(group ^ (e // 2 % 2)) * owners + e for e in range(owners)] for group in range(2)
    ]

    def dispatch(rows):
        slots, wide = rows.shape
        return lax.all_to_all(
            rows.reshape(owners, MAIN, wide),
            ("y", "exp"),
            split_axis=0,
            concat_axis=0,
            axis_index_groups=groups,
            tiled=True,
        ).reshape(slots, wide)

    one = dispatch(one)
    far_one = swap(one)
    two = dispatch(two)
    far_two = swap(two)
    early, left_top, right_bottom = lax.optimization_barrier((two, left_top, right_bottom))
    own_a = gate_up(one, early, both)
    own_a, left_top, right_bottom = lax.optimization_barrier((own_a, left_top, right_bottom))
    far_b = swap(own_a)
    beyond = (ring(left_top, 1), ring(right_bottom, -1))
    far_two, far_b, left_bottom, right_top = lax.optimization_barrier(
        (far_two, far_b, left_bottom, right_top)
    )
    far_a = gate_up(far_one, far_two, both)
    own_b = swap(far_a)
    lower = (*here, left_top, left_bottom, right_top, right_bottom, *beyond)
    out = down(place, (own_a, own_b, far_a, far_b), lower)
    back = lax.all_to_all(
        out.reshape(2 * owners, MAIN, out.shape[2]),
        ("y", "exp"),
        split_axis=0,
        concat_axis=0,
        tiled=True,
    ).reshape(out.shape)
    return combine(expert_ids[0], route_weights[0], h_state, back)[None]


def solution(mesh):
    inner = Mesh(mesh.devices.reshape(2, 4, mesh.shape["exp"]), ("y", "x", "exp"))
    ctx = ("y", "x")
    return jax.shard_map(
        per_device,
        mesh=inner,
        in_specs=(
            P("exp", ctx, None),
            P("exp", ctx, None),
            P("exp", ctx, None),
            P("exp", ctx),
            P("exp", ctx, None),
            P(),
            P("exp", ctx, None),
            P("exp", ctx, None),
            P("exp", None, ctx),
            P("exp", None, ctx),
            P("exp", None, ctx),
        ),
        out_specs=P("exp", ctx, None),
        check_vma=False,
    )
```

```python
import functools
import math

import jax
import jax.numpy as jnp
from jax import lax
from jax.experimental import pallas as pl
from jax.experimental.pallas import tpu as pltpu
from jax.sharding import Mesh
from jax.sharding import PartitionSpec as P

HEADS = 32
KV_HEADS = 2
HEAD_DIM = 128
TOP = 8
HALF = HEAD_DIM // 2
STEP_HEADS = 4
FIRST = 6
MAIN = 8

F32 = jnp.float32
BF16 = jnp.bfloat16


def yarn_tables(position_values):
    half = HEAD_DIM // 2
    theta_base = 1000000.0
    factor = 4.0
    trained_span = 32768.0

    def bound_dim(turns):
        return (
            HEAD_DIM * math.log(trained_span / (turns * 2 * math.pi)) / (2 * math.log(theta_base))
        )

    lower = max(math.floor(bound_dim(32.0)), 0)
    upper = min(math.ceil(bound_dim(1.0)), HEAD_DIM - 1)
    pair_index = jnp.arange(half, dtype=jnp.float32)
    extrapolated = jnp.exp(-(2.0 * pair_index / HEAD_DIM) * math.log(theta_base))
    ramp = jnp.clip((pair_index - lower) / max(upper - lower, 1), 0.0, 1.0)
    inverse = extrapolated / factor * ramp + extrapolated * (1.0 - ramp)
    magnitude = 0.1 * math.log(factor) + 1.0
    angles = position_values.astype(jnp.float32)[..., None] * inverse
    return (jnp.cos(angles) * magnitude, jnp.sin(angles) * magnitude)


def iota(shape, dim):
    return lax.broadcasted_iota(jnp.int32, shape, dim)


def dot(a, b):
    return jnp.dot(a, b, preferred_element_type=F32)


def rotate(head, cos2, sin2):
    return (head * cos2 + pltpu.roll(head, HALF, 1) * sin2).astype(BF16)


def params(mib):
    return pltpu.CompilerParams(vmem_limit_bytes=mib * 2**20)


def kv_kernel(k_ref, v_ref, cos_ref, sin_ref, kv_ref):
    for head in range(KV_HEADS):
        cols = slice(head * HEAD_DIM, (head + 1) * HEAD_DIM)
        kv_ref[:, cols] = rotate(k_ref[:, cols].astype(F32), cos_ref[...], sin_ref[...])
    kv_ref[:, KV_HEADS * HEAD_DIM :] = v_ref[...]


def pack_kv(keys, values, cos2, sin2):
    tokens, width = keys.shape
    return pl.pallas_call(
        kv_kernel,
        out_shape=jax.ShapeDtypeStruct((tokens, 2 * width), BF16),
        name="pack_kv",
    )(keys, values, cos2, sin2)


def pack_weights_kernel(gate_ref, upper_ref, out_ref):
    both = jnp.concatenate(
        [gate_ref[:128], upper_ref[:128], gate_ref[128:], upper_ref[128:]], axis=0
    )
    out_ref[...] = both.T


def pack_weights(gate, upper):
    units, width = gate.shape
    block = width // 4
    return pl.pallas_call(
        pack_weights_kernel,
        grid=(width // block,),
        in_specs=[pl.BlockSpec((units, block), lambda i: (0, i))] * 2,
        out_specs=pl.BlockSpec((block, 2 * units), lambda i: (i, 0)),
        out_shape=jax.ShapeDtypeStruct((width, 2 * units), BF16),
        name="pack_weights",
    )(gate, upper)


def slot_ranks_by_expert(ids_t, experts):
    tokens = ids_t.shape[1]
    expert = iota((experts, tokens), 0)
    named = jnp.zeros((experts, tokens), F32)
    for choice in range(TOP):
        named += (ids_t[choice : choice + 1, :] == expert).astype(F32)
    earlier = (iota((tokens, tokens), 0) < iota((tokens, tokens), 1)).astype(F32)
    rank = dot(named.astype(BF16), earlier.astype(BF16))
    return jnp.where(named > 0.5, rank, 255.0)


def attend_kernel(
    place_ref, q_ref, own_k_ref, own_v_ref, far_k_ref, far_v_ref, cos_ref, sin_ref, residual_ref,
    gain_ref, ids_ref, h_ref, one_ref, two_ref,
):
    step = pl.program_id(0)
    tokens = q_ref.shape[0]
    width = h_ref.shape[1]
    cols = STEP_HEADS * HEAD_DIM
    scale = math.log2(math.e) / math.sqrt(HEAD_DIM)
    pieces = []
    for head in range(STEP_HEADS):
        part = q_ref[:, head * HEAD_DIM : (head + 1) * HEAD_DIM].astype(F32)
        pieces.append(rotate(part, cos_ref[...], sin_ref[...]))
    q_rot = jnp.concatenate(pieces, axis=0)
    contract = (((1,), (1,)), ((), ()))
    near = lax.dot_general(q_rot, own_k_ref[...], contract, preferred_element_type=F32)
    far = lax.dot_general(q_rot, far_k_ref[...], contract, preferred_element_type=F32)
    keys = near.shape[1]
    token = iota(near.shape, 0) % tokens
    limit = place_ref[1] * tokens + token
    near = jnp.where(iota(near.shape, 1) <= limit, near, -1e30)
    far = jnp.where(place_ref[0] > 0, far, jnp.full_like(far, -1e30))
    largest = jnp.maximum(
        jnp.max(near, axis=1, keepdims=True), jnp.max(far, axis=1, keepdims=True)
    )
    near = jnp.exp2((near - largest) * scale)
    far = jnp.exp2((far - largest) * scale)
    total = jnp.sum(near, axis=1, keepdims=True) + jnp.sum(far, axis=1, keepdims=True)
    mixed = dot(near.astype(BF16), own_v_ref[...]) + dot(far.astype(BF16), far_v_ref[...])
    attn = mixed / total
    for head in range(STEP_HEADS):
        here = slice(head * HEAD_DIM, (head + 1) * HEAD_DIM)
        start = pl.multiple_of(step * cols + head * HEAD_DIM, HEAD_DIM)
        h_ref[:, pl.ds(start, HEAD_DIM)] = (
            residual_ref[:, here].astype(F32) + attn[head * tokens : (head + 1) * tokens]
        )

    @pl.when(step == pl.num_programs(0) - 1)
    def _():
        slots, first = one_ref.shape
        experts = slots // MAIN
        ranks = slot_ranks_by_expert(ids_ref[...], experts)
        spread = (iota((slots, experts), 0) // MAIN == iota((slots, experts), 1)).astype(F32)
        at = dot(spread.astype(BF16), ranks.astype(BF16))
        sub = iota((slots, tokens), 0) % MAIN
        main = (at == sub.astype(F32)).astype(F32).astype(BF16)
        last = at == float(MAIN)
        block = width // MAIN
        square = jnp.zeros((tokens, 1), F32)
        for part in range(MAIN):
            piece = h_ref[:, part * block : (part + 1) * block]
            square += jnp.sum(piece * piece, axis=1, keepdims=True)
        norm = 1.0 / jnp.sqrt(square / width + 1e-06)
        folded = jnp.zeros((slots, block), F32)
        for part in range(MAIN):
            here = slice(part * block, (part + 1) * block)
            normed = (h_ref[:, here] * norm * gain_ref[:, here]).astype(BF16)
            sent = dot(main, normed).astype(BF16)
            if (part + 1) * block <= first:
                one_ref[:, here] = sent
            else:
                two_ref[:, part * block - first : (part + 1) * block - first] = sent
            ninth = (last & (sub == part)).astype(F32).astype(BF16)
            folded += dot(ninth, normed)
        two_ref[:, width - first :] = folded.astype(BF16)


def attend(place, queries, own_kv, far_kv, cos2, sin2, residual, gain, ids_t, experts):
    tokens, width = queries.shape
    cols = STEP_HEADS * HEAD_DIM
    steps = width // cols
    per_kv = steps // KV_HEADS
    near = own_kv.shape[0]
    block = width // MAIN
    first = FIRST * block
    whole = lambda shape: pl.BlockSpec(shape, lambda i, place: (0,) * len(shape))
    return pl.pallas_call(
        attend_kernel,
        grid_spec=pltpu.PrefetchScalarGridSpec(
            num_scalar_prefetch=1,
            grid=(steps,),
            in_specs=[
                pl.BlockSpec((tokens, cols), lambda i, place: (0, i)),
                pl.BlockSpec((near, HEAD_DIM), lambda i, place: (0, i // per_kv)),
                pl.BlockSpec((near, HEAD_DIM), lambda i, place: (0, KV_HEADS + i // per_kv)),
                pl.BlockSpec((near, HEAD_DIM), lambda i, place: (0, i // per_kv)),
                pl.BlockSpec((near, HEAD_DIM), lambda i, place: (0, KV_HEADS + i // per_kv)),
                whole((tokens, HEAD_DIM)),
                whole((tokens, HEAD_DIM)),
                pl.BlockSpec((tokens, cols), lambda i, place: (0, i)),
                whole((1, width)),
                whole((TOP, tokens)),
            ],
            out_specs=[
                whole((tokens, width)),
                whole((experts * MAIN, first)),
                whole((experts * MAIN, width + block - first)),
            ],
        ),
        out_shape=[
            jax.ShapeDtypeStruct((tokens, width), F32),
            jax.ShapeDtypeStruct((experts * MAIN, first), BF16),
            jax.ShapeDtypeStruct((experts * MAIN, width + block - first), BF16),
        ],
        compiler_params=params(48),
        name="attend",
    )(place, queries, own_kv, own_kv, far_kv, far_kv, cos2, sin2, residual, gain, ids_t)


def gate_up_kernel(one_ref, two_ref, weights_ref, act_ref, x_ref, tail_ref):
    slots, first = one_ref.shape
    width = x_ref.shape[1]
    experts = slots // MAIN
    block = width // MAIN
    step = pl.program_id(0)

    @pl.when(step == 0)
    def _():
        x_ref[:slots, :first] = one_ref[...]
        x_ref[:slots, first:] = two_ref[:, : width - first]
        folded = two_ref[:, width - first :]
        row, col = iota((experts, slots), 0), iota((experts, slots), 1)
        for part in range(MAIN):
            pick = (col == row * MAIN + part).astype(F32).astype(BF16)
            x_ref[slots:, part * block : (part + 1) * block] = dot(pick, folded).astype(BF16)

    both = dot(x_ref[...], weights_ref[0])
    gated = (silu(both[:, :128]) * both[:, 128:256]).astype(BF16)
    tail = silu(both[:, 256:]) * pltpu.roll(both[:, 256:], HALF, 1)

    @pl.when(step % 2 == 0)
    def _():
        act_ref[:, :128] = gated
        tail_ref[...] = tail

    @pl.when(step % 2 == 1)
    def _():
        act_ref[:, 128:256] = gated
        lane = iota(tail.shape, 1)
        act_ref[:, 256:] = jnp.where(lane < HALF, tail_ref[...], pltpu.roll(tail, HALF, 1)).astype(
            BF16
        )


def silu(v):
    return v / (1.0 + jnp.exp(-v))


def gate_up(one, two, weights):
    slots = one.shape[0]
    shards, width, cols = weights.shape
    total = slots + slots // MAIN
    return pl.pallas_call(
        gate_up_kernel,
        grid=(shards,),
        in_specs=[
            pl.BlockSpec(one.shape, lambda i: (0, 0)),
            pl.BlockSpec(two.shape, lambda i: (0, 0)),
            pl.BlockSpec((1, width, cols), lambda i: (i, 0, 0)),
        ],
        out_specs=pl.BlockSpec((total, cols), lambda i: (0, i // 2)),
        out_shape=jax.ShapeDtypeStruct((total, cols * shards // 2), BF16),
        scratch_shapes=[pltpu.VMEM((total, width), BF16), pltpu.VMEM((total, 128), F32)],
        compiler_params=params(32),
        cost_estimate=pl.CostEstimate(
            flops=2 * total * width * cols * shards,
            bytes_accessed=2 * weights.size + 2 * (one.size + two.size),
            transcendentals=0,
        ),
        name="gate_up",
    )(one, two, weights)


def down_kernel(
    place_ref, own_a, own_b, far_a, far_b, *refs,
):
    weights, (out_ref, act_ref, fold_ref) = refs[:-3], refs[-3:]
    step = pl.program_id(0)
    slots = out_ref.shape[1]
    experts = slots // MAIN
    total = slots + experts
    cols = weights[0].shape[1]
    piece = fold_ref.shape[2]
    shards = (out_ref.shape[2] - piece) // cols

    @pl.when(step == 0)
    def _():
        row = iota((total, 1), 0)
        block = jnp.where(row < slots, row // MAIN, row - slots)
        mine = (block // 2) % 2 == place_ref[2]
        for half, own, far in ((place_ref[0], own_a, far_a), (1 - place_ref[0], own_b, far_b)):
            near, away = own[...].astype(F32), far[...].astype(F32)
            act_ref[half, :total] = jnp.where(mine, near, away).astype(BF16)
            act_ref[half, total:] = jnp.where(mine, away, near).astype(BF16)
        fold_ref[...] = jnp.zeros_like(fold_ref)

    def in_order(weights):
        rows = []
        for base in range(0, weights.shape[0], 384):
            for start, size in ((0, 128), (192, 128), (128, 64), (320, 64)):
                rows.append(weights[base + start : base + start + size])
        return jnp.concatenate(rows, axis=0)

    def multiply(top, bottom, shard):
        y = dot(act_ref[0], in_order(top)) + dot(act_ref[1], in_order(bottom))
        y = y.astype(BF16)
        start = pl.multiple_of(shard * cols, 128)
        row, col = iota((slots, experts), 0), iota((slots, experts), 1)
        for to in range(2):
            out_ref[to, :, pl.ds(start, cols)] = y[to * total : to * total + slots]
            ninth = y[to * total + slots : (to + 1) * total]
            for part in range(cols // piece):
                at = shard * (cols // piece) + part
                put = (row == col * MAIN + at).astype(F32).astype(BF16)
                fold_ref[to] += dot(put, ninth[:, part * piece : (part + 1) * piece])

    for number, ahead in enumerate((0, shards - 1, 1, 2)):

        @pl.when(step == number)
        def _(number=number, ahead=ahead):
            top, bottom = weights[2 * number : 2 * number + 2]
            multiply(top[...], bottom[...], (place_ref[1] + ahead) % shards)

    @pl.when(step == shards - 1)
    def _():
        for to in range(2):
            out_ref[to, :, out_ref.shape[2] - piece :] = fold_ref[to].astype(BF16)


def down(place, acts, weights):
    total, half = acts[0].shape
    cols = weights[0].shape[1]
    shards = len(weights) // 2
    slots = total * MAIN // (MAIN + 1)
    piece = shards * cols // MAIN
    whole = lambda shape: pl.BlockSpec(shape, lambda i, place: (0,) * len(shape))
    return pl.pallas_call(
        down_kernel,
        grid_spec=pltpu.PrefetchScalarGridSpec(
            num_scalar_prefetch=1,
            grid=(shards,),
            in_specs=[whole(a.shape) for a in (*acts, *weights)],
            out_specs=whole((2, slots, shards * cols + piece)),
            scratch_shapes=[
                pltpu.VMEM((2, 2 * total, half), BF16),
                pltpu.VMEM((2, slots, piece), F32),
            ],
        ),
        out_shape=jax.ShapeDtypeStruct((2, slots, shards * cols + piece), BF16),
        compiler_params=params(36),
        name="down",
    )(place, *acts, *weights)


def combine_kernel(ids_ref, weights_ref, h_ref, back_ref, out_ref):
    tokens = h_ref.shape[0]
    slots = back_ref.shape[1]
    experts = slots // MAIN
    width = h_ref.shape[1]
    piece = width // MAIN
    expert = iota((tokens, experts), 1)
    named = jnp.zeros((tokens, experts), F32)
    weight = jnp.zeros((tokens, experts), F32)
    for choice in range(TOP):
        match = ids_ref[:, choice : choice + 1] == expert
        named += match.astype(F32)
        weight += jnp.where(match, weights_ref[:, choice : choice + 1], 0.0)
    earlier = (iota((tokens, tokens), 1) < iota((tokens, tokens), 0)).astype(F32)
    rank = jnp.where(named > 0.5, dot(earlier.astype(BF16), named.astype(BF16)), 255.0)
    spread = (iota((experts, slots), 1) // MAIN == iota((experts, slots), 0)).astype(F32)
    spread = spread.astype(BF16)
    at = dot(rank.astype(BF16), spread)
    sub = iota((tokens, slots), 1) % MAIN
    levels = []
    rest = weight
    for _ in range(3):
        level = rest.astype(BF16)
        rest = rest - level.astype(F32)
        levels.append(dot(level, spread))
    main = [jnp.where(at == sub.astype(F32), level, 0.0).astype(BF16) for level in levels]
    last = [jnp.where(at == float(MAIN), level, 0.0) for level in levels]
    main = jnp.concatenate(main, axis=0)

    def add_up(stacked):
        return stacked[:tokens] + (stacked[tokens : 2 * tokens] + stacked[2 * tokens :])

    for part in range(MAIN):
        here = slice(part * piece, (part + 1) * piece)
        ninth = jnp.concatenate(
            [jnp.where(sub == part, level, 0.0).astype(BF16) for level in last], axis=0
        )
        summed = dot(main, back_ref[0, :, here]) + dot(ninth, back_ref[0, :, width:])
        out_ref[:, here] = (h_ref[:, here] + add_up(summed)).astype(BF16)


def combine(ids, weights, h_state, back):
    tokens, width = h_state.shape
    halves, slots, wide = back.shape
    part = width // halves
    return pl.pallas_call(
        combine_kernel,
        grid=(halves,),
        in_specs=[
            pl.BlockSpec((tokens, TOP), lambda i: (0, 0)),
            pl.BlockSpec((tokens, TOP), lambda i: (0, 0)),
            pl.BlockSpec((tokens, part), lambda i: (0, i)),
            pl.BlockSpec((1, slots, wide), lambda i: (i, 0, 0)),
        ],
        out_specs=pl.BlockSpec((tokens, part), lambda i: (0, i)),
        out_shape=jax.ShapeDtypeStruct((tokens, width), BF16),
        compiler_params=params(48),
        name="combine",
    )(ids, weights, h_state, back)


def swap(x):
    return lax.ppermute(x, "y", [(0, 1), (1, 0)])


def ring(x, ahead):
    return lax.ppermute(x, "x", [(i, (i + ahead) % 4) for i in range(4)])


def per_device(
    queries,
    keys,
    values,
    positions,
    residual,
    norm_gain,
    expert_ids,
    route_weights,
    w_gate,
    w_up,
    w_down,
):
    width = queries.shape[2]
    owners = lax.axis_size("exp")
    y_high = (lax.axis_index("exp") >> 1) & 1
    place = jnp.stack([lax.axis_index("y"), lax.axis_index("x"), lax.axis_index("y") ^ y_high])
    place = place.astype(jnp.int32)

    cosine, sine = yarn_tables(positions[0])
    cos2 = jnp.concatenate([cosine, cosine], axis=1)
    sin2 = jnp.concatenate([-sine, sine], axis=1)
    kv = pack_kv(keys[0], values[0], cos2, sin2)
    own_kv = lax.all_gather(kv, "x", axis=0, tiled=True)
    far_kv = lax.ppermute(own_kv, "y", [(0, 1)])

    both = pack_weights(w_gate[0].T, w_up[0].T)
    both = lax.all_gather(both, "x", axis=0, tiled=True).reshape(4, width, both.shape[1])
    hidden, cols = w_down.shape[1:]
    here = (w_down[0, : hidden // 2], w_down[0, hidden // 2 :])
    left_top, right_bottom = ring(here[0], 1), ring(here[1], -1)
    left_bottom, right_top = ring(here[1], 1), ring(here[0], -1)

    h_state, one, two = attend(
        place, queries[0], own_kv, far_kv, cos2, sin2, residual[0], norm_gain[None],
        expert_ids[0].T, owners,
    )

    groups = [
        [(group ^ (e // 2 % 2)) * owners + e for e in range(owners)] for group in range(2)
    ]

    def dispatch(rows):
        slots, wide = rows.shape
        return lax.all_to_all(
            rows.reshape(owners, MAIN, wide),
            ("y", "exp"),
            split_axis=0,
            concat_axis=0,
            axis_index_groups=groups,
            tiled=True,
        ).reshape(slots, wide)

    one = dispatch(one)
    far_one = swap(one)
    two = dispatch(two)
    far_two = swap(two)
    early, left_top, right_bottom = lax.optimization_barrier((two, left_top, right_bottom))
    own_a = gate_up(one, early, both)
    own_a, left_top, right_bottom = lax.optimization_barrier((own_a, left_top, right_bottom))
    far_b = swap(own_a)
    beyond = (ring(left_top, 1), ring(right_bottom, -1))
    far_two, far_b, left_bottom, right_top = lax.optimization_barrier(
        (far_two, far_b, left_bottom, right_top)
    )
    far_a = gate_up(far_one, far_two, both)
    own_b = swap(far_a)
    lower = (*here, left_top, left_bottom, right_top, right_bottom, *beyond)
    out = down(place, (own_a, own_b, far_a, far_b), lower)
    back = lax.all_to_all(
        out.reshape(2 * owners, MAIN, out.shape[2]),
        ("y", "exp"),
        split_axis=0,
        concat_axis=0,
        tiled=True,
    ).reshape(out.shape)
    return combine(expert_ids[0], route_weights[0], h_state, back)[None]


def solution(mesh):
    inner = Mesh(mesh.devices.reshape(2, 4, mesh.shape["exp"]), ("y", "x", "exp"))
    ctx = ("y", "x")
    return jax.shard_map(
        per_device,
        mesh=inner,
        in_specs=(
            P("exp", ctx, None),
            P("exp", ctx, None),
            P("exp", ctx, None),
            P("exp", ctx),
            P("exp", ctx, None),
            P(),
            P("exp", ctx, None),
            P("exp", ctx, None),
            P("exp", None, ctx),
            P("exp", None, ctx),
            P("exp", None, ctx),
        ),
        out_specs=P("exp", ctx, None),
        check_vma=False,
    )
```

```python
import functools
import math

import jax
import jax.numpy as jnp
from jax import lax
from jax.experimental import pallas as pl
from jax.experimental.pallas import tpu as pltpu
from jax.sharding import Mesh
from jax.sharding import PartitionSpec as P

HEADS = 32
KV_HEADS = 2
HEAD_DIM = 128
TOP = 8
HALF = HEAD_DIM // 2
STEP_HEADS = 4
FIRST = 5
MAIN = 8

F32 = jnp.float32
BF16 = jnp.bfloat16


def yarn_tables(position_values):
    half = HEAD_DIM // 2
    theta_base = 1000000.0
    factor = 4.0
    trained_span = 32768.0

    def bound_dim(turns):
        return (
            HEAD_DIM * math.log(trained_span / (turns * 2 * math.pi)) / (2 * math.log(theta_base))
        )

    lower = max(math.floor(bound_dim(32.0)), 0)
    upper = min(math.ceil(bound_dim(1.0)), HEAD_DIM - 1)
    pair_index = jnp.arange(half, dtype=jnp.float32)
    extrapolated = jnp.exp(-(2.0 * pair_index / HEAD_DIM) * math.log(theta_base))
    ramp = jnp.clip((pair_index - lower) / max(upper - lower, 1), 0.0, 1.0)
    inverse = extrapolated / factor * ramp + extrapolated * (1.0 - ramp)
    magnitude = 0.1 * math.log(factor) + 1.0
    angles = position_values.astype(jnp.float32)[..., None] * inverse
    return (jnp.cos(angles) * magnitude, jnp.sin(angles) * magnitude)


def iota(shape, dim):
    return lax.broadcasted_iota(jnp.int32, shape, dim)


def dot(a, b):
    return jnp.dot(a, b, preferred_element_type=F32)


def rotate(head, cos2, sin2):
    return (head * cos2 + pltpu.roll(head, HALF, 1) * sin2).astype(BF16)


def params(mib):
    return pltpu.CompilerParams(vmem_limit_bytes=mib * 2**20)


def kv_kernel(k_ref, v_ref, cos_ref, sin_ref, kv_ref):
    for head in range(KV_HEADS):
        cols = slice(head * HEAD_DIM, (head + 1) * HEAD_DIM)
        kv_ref[:, cols] = rotate(k_ref[:, cols].astype(F32), cos_ref[...], sin_ref[...])
    kv_ref[:, KV_HEADS * HEAD_DIM :] = v_ref[...]


def pack_kv(keys, values, cos2, sin2):
    tokens, width = keys.shape
    return pl.pallas_call(
        kv_kernel,
        out_shape=jax.ShapeDtypeStruct((tokens, 2 * width), BF16),
        name="pack_kv",
    )(keys, values, cos2, sin2)


def pack_weights_kernel(gate_ref, upper_ref, out_ref):
    both = jnp.concatenate(
        [gate_ref[:128], upper_ref[:128], gate_ref[128:], upper_ref[128:]], axis=0
    )
    out_ref[...] = both.T


def pack_weights(gate, upper):
    units, width = gate.shape
    block = width // 4
    return pl.pallas_call(
        pack_weights_kernel,
        grid=(width // block,),
        in_specs=[pl.BlockSpec((units, block), lambda i: (0, i))] * 2,
        out_specs=pl.BlockSpec((block, 2 * units), lambda i: (i, 0)),
        out_shape=jax.ShapeDtypeStruct((width, 2 * units), BF16),
        name="pack_weights",
    )(gate, upper)


def slot_ranks_by_expert(ids_t, experts):
    tokens = ids_t.shape[1]
    expert = iota((experts, tokens), 0)
    named = jnp.zeros((experts, tokens), F32)
    for choice in range(TOP):
        named += (ids_t[choice : choice + 1, :] == expert).astype(F32)
    earlier = (iota((tokens, tokens), 0) < iota((tokens, tokens), 1)).astype(F32)
    rank = dot(named.astype(BF16), earlier.astype(BF16))
    return jnp.where(named > 0.5, rank, 255.0)


def attend_kernel(
    place_ref, q_ref, own_k_ref, own_v_ref, far_k_ref, far_v_ref, cos_ref, sin_ref, residual_ref,
    gain_ref, ids_ref, h_ref, one_ref, two_ref,
):
    step = pl.program_id(0)
    tokens = q_ref.shape[0]
    width = h_ref.shape[1]
    cols = STEP_HEADS * HEAD_DIM
    scale = math.log2(math.e) / math.sqrt(HEAD_DIM)
    pieces = []
    for head in range(STEP_HEADS):
        part = q_ref[:, head * HEAD_DIM : (head + 1) * HEAD_DIM].astype(F32)
        pieces.append(rotate(part, cos_ref[...], sin_ref[...]))
    q_rot = jnp.concatenate(pieces, axis=0)
    contract = (((1,), (1,)), ((), ()))
    near = lax.dot_general(q_rot, own_k_ref[...], contract, preferred_element_type=F32)
    far = lax.dot_general(q_rot, far_k_ref[...], contract, preferred_element_type=F32)
    keys = near.shape[1]
    token = iota(near.shape, 0) % tokens
    limit = place_ref[1] * tokens + token
    near = jnp.where(iota(near.shape, 1) <= limit, near, -1e30)
    far = jnp.where(place_ref[0] > 0, far, jnp.full_like(far, -1e30))
    largest = jnp.maximum(
        jnp.max(near, axis=1, keepdims=True), jnp.max(far, axis=1, keepdims=True)
    )
    near = jnp.exp2((near - largest) * scale)
    far = jnp.exp2((far - largest) * scale)
    total = jnp.sum(near, axis=1, keepdims=True) + jnp.sum(far, axis=1, keepdims=True)
    mixed = dot(near.astype(BF16), own_v_ref[...]) + dot(far.astype(BF16), far_v_ref[...])
    attn = mixed / total
    for head in range(STEP_HEADS):
        here = slice(head * HEAD_DIM, (head + 1) * HEAD_DIM)
        start = pl.multiple_of(step * cols + head * HEAD_DIM, HEAD_DIM)
        h_ref[:, pl.ds(start, HEAD_DIM)] = (
            residual_ref[:, here].astype(F32) + attn[head * tokens : (head + 1) * tokens]
        )

    @pl.when(step == pl.num_programs(0) - 1)
    def _():
        slots, first = one_ref.shape
        experts = slots // MAIN
        ranks = slot_ranks_by_expert(ids_ref[...], experts)
        spread = (iota((slots, experts), 0) // MAIN == iota((slots, experts), 1)).astype(F32)
        at = dot(spread.astype(BF16), ranks.astype(BF16))
        sub = iota((slots, tokens), 0) % MAIN
        main = (at == sub.astype(F32)).astype(F32).astype(BF16)
        last = at == float(MAIN)
        block = width // MAIN
        square = jnp.zeros((tokens, 1), F32)
        for part in range(MAIN):
            piece = h_ref[:, part * block : (part + 1) * block]
            square += jnp.sum(piece * piece, axis=1, keepdims=True)
        norm = 1.0 / jnp.sqrt(square / width + 1e-06)
        folded = jnp.zeros((slots, block), F32)
        for part in range(MAIN):
            here = slice(part * block, (part + 1) * block)
            normed = (h_ref[:, here] * norm * gain_ref[:, here]).astype(BF16)
            sent = dot(main, normed).astype(BF16)
            if (part + 1) * block <= first:
                one_ref[:, here] = sent
            else:
                two_ref[:, part * block - first : (part + 1) * block - first] = sent
            ninth = (last & (sub == part)).astype(F32).astype(BF16)
            folded += dot(ninth, normed)
        two_ref[:, width - first :] = folded.astype(BF16)


def attend(place, queries, own_kv, far_kv, cos2, sin2, residual, gain, ids_t, experts):
    tokens, width = queries.shape
    cols = STEP_HEADS * HEAD_DIM
    steps = width // cols
    per_kv = steps // KV_HEADS
    near = own_kv.shape[0]
    block = width // MAIN
    first = FIRST * block
    whole = lambda shape: pl.BlockSpec(shape, lambda i, place: (0,) * len(shape))
    return pl.pallas_call(
        attend_kernel,
        grid_spec=pltpu.PrefetchScalarGridSpec(
            num_scalar_prefetch=1,
            grid=(steps,),
            in_specs=[
                pl.BlockSpec((tokens, cols), lambda i, place: (0, i)),
                pl.BlockSpec((near, HEAD_DIM), lambda i, place: (0, i // per_kv)),
                pl.BlockSpec((near, HEAD_DIM), lambda i, place: (0, KV_HEADS + i // per_kv)),
                pl.BlockSpec((near, HEAD_DIM), lambda i, place: (0, i // per_kv)),
                pl.BlockSpec((near, HEAD_DIM), lambda i, place: (0, KV_HEADS + i // per_kv)),
                whole((tokens, HEAD_DIM)),
                whole((tokens, HEAD_DIM)),
                pl.BlockSpec((tokens, cols), lambda i, place: (0, i)),
                whole((1, width)),
                whole((TOP, tokens)),
            ],
            out_specs=[
                whole((tokens, width)),
                whole((experts * MAIN, first)),
                whole((experts * MAIN, width + block - first)),
            ],
        ),
        out_shape=[
            jax.ShapeDtypeStruct((tokens, width), F32),
            jax.ShapeDtypeStruct((experts * MAIN, first), BF16),
            jax.ShapeDtypeStruct((experts * MAIN, width + block - first), BF16),
        ],
        compiler_params=params(48),
        name="attend",
    )(place, queries, own_kv, own_kv, far_kv, far_kv, cos2, sin2, residual, gain, ids_t)


def gate_up_kernel(one_ref, two_ref, weights_ref, act_ref, x_ref, tail_ref):
    slots, first = one_ref.shape
    width = x_ref.shape[1]
    experts = slots // MAIN
    block = width // MAIN
    step = pl.program_id(0)

    @pl.when(step == 0)
    def _():
        x_ref[:slots, :first] = one_ref[...]
        x_ref[:slots, first:] = two_ref[:, : width - first]
        folded = two_ref[:, width - first :]
        row, col = iota((experts, slots), 0), iota((experts, slots), 1)
        for part in range(MAIN):
            pick = (col == row * MAIN + part).astype(F32).astype(BF16)
            x_ref[slots:, part * block : (part + 1) * block] = dot(pick, folded).astype(BF16)

    both = dot(x_ref[...], weights_ref[0])
    gated = (silu(both[:, :128]) * both[:, 128:256]).astype(BF16)
    tail = silu(both[:, 256:]) * pltpu.roll(both[:, 256:], HALF, 1)

    @pl.when(step % 2 == 0)
    def _():
        act_ref[:, :128] = gated
        tail_ref[...] = tail

    @pl.when(step % 2 == 1)
    def _():
        act_ref[:, 128:256] = gated
        lane = iota(tail.shape, 1)
        act_ref[:, 256:] = jnp.where(lane < HALF, tail_ref[...], pltpu.roll(tail, HALF, 1)).astype(
            BF16
        )


def silu(v):
    return v / (1.0 + jnp.exp(-v))


def gate_up(one, two, weights):
    slots = one.shape[0]
    shards, width, cols = weights.shape
    total = slots + slots // MAIN
    return pl.pallas_call(
        gate_up_kernel,
        grid=(shards,),
        in_specs=[
            pl.BlockSpec(one.shape, lambda i: (0, 0)),
            pl.BlockSpec(two.shape, lambda i: (0, 0)),
            pl.BlockSpec((1, width, cols), lambda i: (i, 0, 0)),
        ],
        out_specs=pl.BlockSpec((total, cols), lambda i: (0, i // 2)),
        out_shape=jax.ShapeDtypeStruct((total, cols * shards // 2), BF16),
        scratch_shapes=[pltpu.VMEM((total, width), BF16), pltpu.VMEM((total, 128), F32)],
        compiler_params=params(32),
        cost_estimate=pl.CostEstimate(
            flops=2 * total * width * cols * shards,
            bytes_accessed=2 * weights.size + 2 * (one.size + two.size),
            transcendentals=0,
        ),
        name="gate_up",
    )(one, two, weights)


def down_kernel(
    place_ref, own_a, own_b, far_a, far_b, *refs,
):
    weights, (out_ref, act_ref, fold_ref) = refs[:-3], refs[-3:]
    step = pl.program_id(0)
    slots = out_ref.shape[1]
    experts = slots // MAIN
    total = slots + experts
    cols = weights[0].shape[1]
    piece = fold_ref.shape[2]
    shards = (out_ref.shape[2] - piece) // cols

    @pl.when(step == 0)
    def _():
        row = iota((total, 1), 0)
        block = jnp.where(row < slots, row // MAIN, row - slots)
        mine = (block // 2) % 2 == place_ref[2]
        for half, own, far in ((place_ref[0], own_a, far_a), (1 - place_ref[0], own_b, far_b)):
            near, away = own[...].astype(F32), far[...].astype(F32)
            act_ref[half, :total] = jnp.where(mine, near, away).astype(BF16)
            act_ref[half, total:] = jnp.where(mine, away, near).astype(BF16)
        fold_ref[...] = jnp.zeros_like(fold_ref)

    def in_order(weights):
        rows = []
        for base in range(0, weights.shape[0], 384):
            for start, size in ((0, 128), (192, 128), (128, 64), (320, 64)):
                rows.append(weights[base + start : base + start + size])
        return jnp.concatenate(rows, axis=0)

    def multiply(top, bottom, shard):
        y = dot(act_ref[0], in_order(top)) + dot(act_ref[1], in_order(bottom))
        y = y.astype(BF16)
        start = pl.multiple_of(shard * cols, 128)
        row, col = iota((slots, experts), 0), iota((slots, experts), 1)
        for to in range(2):
            out_ref[to, :, pl.ds(start, cols)] = y[to * total : to * total + slots]
            ninth = y[to * total + slots : (to + 1) * total]
            for part in range(cols // piece):
                at = shard * (cols // piece) + part
                put = (row == col * MAIN + at).astype(F32).astype(BF16)
                fold_ref[to] += dot(put, ninth[:, part * piece : (part + 1) * piece])

    for number, ahead in enumerate((0, shards - 1, 1, 2)):

        @pl.when(step == number)
        def _(number=number, ahead=ahead):
            top, bottom = weights[2 * number : 2 * number + 2]
            multiply(top[...], bottom[...], (place_ref[1] + ahead) % shards)

    @pl.when(step == shards - 1)
    def _():
        for to in range(2):
            out_ref[to, :, out_ref.shape[2] - piece :] = fold_ref[to].astype(BF16)


def down(place, acts, weights):
    total, half = acts[0].shape
    cols = weights[0].shape[1]
    shards = len(weights) // 2
    slots = total * MAIN // (MAIN + 1)
    piece = shards * cols // MAIN
    whole = lambda shape: pl.BlockSpec(shape, lambda i, place: (0,) * len(shape))
    return pl.pallas_call(
        down_kernel,
        grid_spec=pltpu.PrefetchScalarGridSpec(
            num_scalar_prefetch=1,
            grid=(shards,),
            in_specs=[whole(a.shape) for a in (*acts, *weights)],
            out_specs=whole((2, slots, shards * cols + piece)),
            scratch_shapes=[
                pltpu.VMEM((2, 2 * total, half), BF16),
                pltpu.VMEM((2, slots, piece), F32),
            ],
        ),
        out_shape=jax.ShapeDtypeStruct((2, slots, shards * cols + piece), BF16),
        compiler_params=params(36),
        name="down",
    )(place, *acts, *weights)


def combine_kernel(ids_ref, weights_ref, h_ref, back_ref, out_ref):
    tokens = h_ref.shape[0]
    slots = back_ref.shape[1]
    experts = slots // MAIN
    width = h_ref.shape[1]
    piece = width // MAIN
    expert = iota((tokens, experts), 1)
    named = jnp.zeros((tokens, experts), F32)
    weight = jnp.zeros((tokens, experts), F32)
    for choice in range(TOP):
        match = ids_ref[:, choice : choice + 1] == expert
        named += match.astype(F32)
        weight += jnp.where(match, weights_ref[:, choice : choice + 1], 0.0)
    earlier = (iota((tokens, tokens), 1) < iota((tokens, tokens), 0)).astype(F32)
    rank = jnp.where(named > 0.5, dot(earlier.astype(BF16), named.astype(BF16)), 255.0)
    spread = (iota((experts, slots), 1) // MAIN == iota((experts, slots), 0)).astype(F32)
    spread = spread.astype(BF16)
    at = dot(rank.astype(BF16), spread)
    sub = iota((tokens, slots), 1) % MAIN
    levels = []
    rest = weight
    for _ in range(3):
        level = rest.astype(BF16)
        rest = rest - level.astype(F32)
        levels.append(dot(level, spread))
    main = [jnp.where(at == sub.astype(F32), level, 0.0).astype(BF16) for level in levels]
    last = [jnp.where(at == float(MAIN), level, 0.0) for level in levels]
    main = jnp.concatenate(main, axis=0)

    def add_up(stacked):
        return stacked[:tokens] + (stacked[tokens : 2 * tokens] + stacked[2 * tokens :])

    for part in range(MAIN):
        here = slice(part * piece, (part + 1) * piece)
        ninth = jnp.concatenate(
            [jnp.where(sub == part, level, 0.0).astype(BF16) for level in last], axis=0
        )
        summed = dot(main, back_ref[0, :, here]) + dot(ninth, back_ref[0, :, width:])
        out_ref[:, here] = (h_ref[:, here] + add_up(summed)).astype(BF16)


def combine(ids, weights, h_state, back):
    tokens, width = h_state.shape
    halves, slots, wide = back.shape
    part = width // halves
    return pl.pallas_call(
        combine_kernel,
        grid=(halves,),
        in_specs=[
            pl.BlockSpec((tokens, TOP), lambda i: (0, 0)),
            pl.BlockSpec((tokens, TOP), lambda i: (0, 0)),
            pl.BlockSpec((tokens, part), lambda i: (0, i)),
            pl.BlockSpec((1, slots, wide), lambda i: (i, 0, 0)),
        ],
        out_specs=pl.BlockSpec((tokens, part), lambda i: (0, i)),
        out_shape=jax.ShapeDtypeStruct((tokens, width), BF16),
        compiler_params=params(48),
        name="combine",
    )(ids, weights, h_state, back)


def swap(x):
    return lax.ppermute(x, "y", [(0, 1), (1, 0)])


def ring(x, ahead):
    return lax.ppermute(x, "x", [(i, (i + ahead) % 4) for i in range(4)])


def per_device(
    queries,
    keys,
    values,
    positions,
    residual,
    norm_gain,
    expert_ids,
    route_weights,
    w_gate,
    w_up,
    w_down,
):
    width = queries.shape[2]
    owners = lax.axis_size("exp")
    y_high = (lax.axis_index("exp") >> 1) & 1
    place = jnp.stack([lax.axis_index("y"), lax.axis_index("x"), lax.axis_index("y") ^ y_high])
    place = place.astype(jnp.int32)

    cosine, sine = yarn_tables(positions[0])
    cos2 = jnp.concatenate([cosine, cosine], axis=1)
    sin2 = jnp.concatenate([-sine, sine], axis=1)
    kv = pack_kv(keys[0], values[0], cos2, sin2)
    own_kv = lax.all_gather(kv, "x", axis=0, tiled=True)
    far_kv = lax.ppermute(own_kv, "y", [(0, 1)])

    both = pack_weights(w_gate[0].T, w_up[0].T)
    both = lax.all_gather(both, "x", axis=0, tiled=True).reshape(4, width, both.shape[1])
    hidden, cols = w_down.shape[1:]
    h_state, one, two = attend(
        place, queries[0], own_kv, far_kv, cos2, sin2, residual[0], norm_gain[None],
        expert_ids[0].T, owners,
    )

    groups = [
        [(group ^ (e // 2 % 2)) * owners + e for e in range(owners)] for group in range(2)
    ]

    def dispatch(rows):
        slots, wide = rows.shape
        return lax.all_to_all(
            rows.reshape(owners, MAIN, wide),
            ("y", "exp"),
            split_axis=0,
            concat_axis=0,
            axis_index_groups=groups,
            tiled=True,
        ).reshape(slots, wide)

    one = dispatch(one)
    far_one = swap(one)
    two = dispatch(two)
    two, lower = lax.optimization_barrier((two, w_down[0]))
    far_two = swap(two)
    here = (lower[: hidden // 2], lower[hidden // 2 :])
    left_top, right_bottom = ring(here[0], 1), ring(here[1], -1)
    left_bottom, right_top = ring(here[1], 1), ring(here[0], -1)
    own_a = gate_up(one, two, both)
    far_b = swap(own_a)
    far_two, far_b, left_top, right_bottom, left_bottom, right_top = lax.optimization_barrier(
        (far_two, far_b, left_top, right_bottom, left_bottom, right_top)
    )
    beyond = (ring(left_top, 1), ring(right_bottom, -1))
    far_a = gate_up(far_one, far_two, both)
    own_b = swap(far_a)
    lower = (*here, left_top, left_bottom, right_top, right_bottom, *beyond)
    out = down(place, (own_a, own_b, far_a, far_b), lower)
    back = lax.all_to_all(
        out.reshape(2 * owners, MAIN, out.shape[2]),
        ("y", "exp"),
        split_axis=0,
        concat_axis=0,
        tiled=True,
    ).reshape(out.shape)
    return combine(expert_ids[0], route_weights[0], h_state, back)[None]


def solution(mesh):
    inner = Mesh(mesh.devices.reshape(2, 4, mesh.shape["exp"]), ("y", "x", "exp"))
    ctx = ("y", "x")
    return jax.shard_map(
        per_device,
        mesh=inner,
        in_specs=(
            P("exp", ctx, None),
            P("exp", ctx, None),
            P("exp", ctx, None),
            P("exp", ctx),
            P("exp", ctx, None),
            P(),
            P("exp", ctx, None),
            P("exp", ctx, None),
            P("exp", None, ctx),
            P("exp", None, ctx),
            P("exp", None, ctx),
        ),
        out_specs=P("exp", ctx, None),
        check_vma=False,
    )
```
